32 devices in a mesh: tm: 8 (over z, y), space: 4 (over x, core).
Axes of the slice: x: 2, y: 2, z: 4, core: 2. Of those that a mesh axis runs over, the one named last changes fastest.
Arguments:
- initial_field: float32 [32, 8, 512], P('space'), may hold values from -1.2 to 1.2
- mobility: float32 [32, 8, 512], P('space'), may hold values from 0.25 to 1
Outputs:
- ends: float32 [8, 32, 8, 512], P('tm', 'space')
The draws below stay inside these ranges and needn't reach their ends.
All inputs are finite; a program needn't handle non-finite values.
Results may differ from the reference program's by a relative error of at most 0.0001.
Values sent between devices are 32-bit elements; how exact they have to be, the bound alone decides.
A program may use at most 64 MiB of HBM per device.

```python
import math
import jax
import jax.numpy as jnp
from jax import lax

NY = 8
NX = 512
ITERS = 2
NZ = 32
N_TM = 8


def level_of(rng, shape, split, smallest, top_value):
    def one(axis_at, parts):
        steps = jax.random.uniform(jax.random.fold_in(jax.random.fold_in(rng, 6), axis_at), (parts,), jnp.float32, smallest / len(split), top_value / len(split))
        return jnp.repeat(jnp.exp(steps), shape[axis_at] // parts).reshape((-1,) + (1,) * (len(shape) - axis_at - 1))

    gain = one(*split[0])
    for cut in split[1:]:
        gain = gain * one(*cut)
    return gain


def setup_inputs(seed: int = 0) -> dict:
    seeds = jax.random.split(jax.random.key(seed), 3)
    return {
        "initial_field": jnp.clip(jax.random.uniform(seeds[0], (NZ, NY, NX), jnp.float32, -1.2, 1.2) * level_of(seeds[0], (NZ, NY, NX), ((0, 4),), -0.4, 0.0), -1.2, 1.2),
        "mobility": jnp.clip(jnp.exp(math.log(1.0) - 1.3862944 * jax.random.uniform(seeds[1], (NZ, NY, NX), jnp.float32) ** level_of(seeds[1], (NZ, NY, NX), ((0, 4),), -0.2, 0.2)), 0.25, 1.0),
    }


gradient_coef = 1.0
slice_step = 0.016
half_step = 0.008
coarse_scale = 0.25


def chemical_flow(values, coefficient, inv_spacing):
    interior = values[..., 1:-1, :, :]
    laplace = (values[..., 2:, :, :] + values[..., :-2, :, :] + jnp.roll(interior, 1, -2) + jnp.roll(interior, -1, -2) + jnp.roll(interior, 1, -1) + jnp.roll(interior, -1, -1) - 6.0 * interior) * inv_spacing
    potential = interior * interior * interior - interior - gradient_coef * laplace
    mobile = coefficient[..., 1:-1, :, :] * jnp.maximum(1.0 - interior * interior, 0.0)
    face_z = 0.5 * (mobile[..., 1:, :, :] + mobile[..., :-1, :, :]) * (potential[..., 1:, :, :] - potential[..., :-1, :, :])
    centre_pot = potential[..., 1:-1, :, :]
    centre_mob = mobile[..., 1:-1, :, :]
    face_y = 0.5 * (jnp.roll(centre_mob, -1, -2) + centre_mob) * (jnp.roll(centre_pot, -1, -2) - centre_pot)
    face_x = 0.5 * (jnp.roll(centre_mob, -1, -1) + centre_mob) * (jnp.roll(centre_pot, -1, -1) - centre_pot)
    summed = (face_z[..., 1:, :, :] - face_z[..., :-1, :, :]) + (face_y - jnp.roll(face_y, 1, -2)) + (face_x - jnp.roll(face_x, 1, -1))
    return summed * inv_spacing


def planar_flow(values, coefficient, inv_spacing):
    laplace = (jnp.roll(values, 1, -2) + jnp.roll(values, -1, -2) + jnp.roll(values, 1, -1) + jnp.roll(values, -1, -1) - 4.0 * values) * inv_spacing
    potential = values * values * values - values - gradient_coef * laplace
    mobile = coefficient * jnp.maximum(1.0 - values * values, 0.0)
    face_y = 0.5 * (jnp.roll(mobile, -1, -2) + mobile) * (jnp.roll(potential, -1, -2) - potential)
    face_x = 0.5 * (jnp.roll(mobile, -1, -1) + mobile) * (jnp.roll(potential, -1, -1) - potential)
    summed = (face_y - jnp.roll(face_y, 1, -2)) + (face_x - jnp.roll(face_x, 1, -1))
    return summed * inv_spacing


def periodic(values, margin):
    return jnp.concatenate([values[..., -margin:, :, :], values, values[..., :margin, :, :]], axis=-3)


def restrict(values):
    leading = values.shape[:-3]
    plane_count, row_count, col_count = values.shape[-3:]
    blocks = values.reshape(leading + (plane_count // 2, 2, row_count // 2, 2, col_count // 2, 2))
    return jnp.sum(blocks, axis=(-5, -3, -1)) * 0.125


def prolong(coarse):
    leading = coarse.shape[:-3]
    plane_count, row_count, col_count = coarse.shape[-3:]
    spread = jnp.broadcast_to(coarse[..., :, None, :, None, :, None], leading + (plane_count, 2, row_count, 2, col_count, 2))
    return spread.reshape(leading + (2 * plane_count, 2 * row_count, 2 * col_count))


def reference(initial_field, mobility):
    slice_count = N_TM
    mobility_wide = periodic(mobility, 2)
    coarse_mobility = restrict(mobility)

    def fine_force(values):
        return chemical_flow(periodic(values, 2), mobility_wide, 1.0)

    def coarse_force(values):
        return planar_flow(values, coarse_mobility, coarse_scale)

    first_force = fine_force(initial_field)
    shape_all = (slice_count,) + initial_field.shape
    node_zero = jnp.broadcast_to(initial_field, shape_all)
    f_zero = jnp.broadcast_to(first_force, shape_all)
    f_one = f_zero
    f_two = f_zero
    node_one = node_zero
    node_two = node_zero
    for sweep_index in range(ITERS):
        if sweep_index > 0:
            f_zero = fine_force(node_zero)
            f_one = fine_force(node_one)
            f_two = fine_force(node_two)
        middle = node_zero + slice_step * ((5.0 / 24.0) * f_zero + (1.0 / 3.0) * f_one - (1.0 / 24.0) * f_two)
        middle_force = fine_force(middle)
        ending = middle + half_step * (middle_force - f_one) + slice_step * (-(1.0 / 24.0) * f_zero + (1.0 / 3.0) * f_one + (5.0 / 24.0) * f_two)
        ending_force = fine_force(ending)
        coarse_zero = restrict(node_zero)
        coarse_one = restrict(ending)
        integral = restrict(slice_step / 6.0 * (f_zero + 4.0 * middle_force + ending_force))
        forcing = integral - slice_step * coarse_force(coarse_zero)

        def chain_step(current, forcing_here):
            advanced = current + slice_step * coarse_force(current) + forcing_here
            return advanced, (current, advanced)

        unused, outputs = lax.scan(chain_step, coarse_zero[0], forcing)
        w_zero, w_one = outputs
        node_one = middle + prolong(0.5 * ((w_zero - coarse_zero) + (w_one - coarse_one)))
        node_two = ending + prolong(w_one - coarse_one)
        if sweep_index + 1 < ITERS:
            node_zero = jnp.concatenate([initial_field[None], node_two[:-1]], axis=0)
    return node_two
```

```python
import functools

import jax
import jax.numpy as jnp
from jax import lax
from jax.experimental import pallas as pl
from jax.experimental.pallas import tpu as pltpu
from jax.sharding import PartitionSpec as P


DT = 0.016
HALO = 12
MESH = pl.DeviceIdType.MESH


def roll(x, shift, axis):
    return pltpu.roll(x, shift % x.shape[axis], axis)


def chem_mob(below, here, above, coef):
    square = here * here
    around = (
        (below + above)
        + (roll(here, 1, 0) + roll(here, -1, 0))
        + (roll(here, 1, 1) + roll(here, -1, 1))
    )
    chem = here * (square + 5.0) - around
    mob = coef * jnp.maximum(1.0 - square, 0.0)
    return chem, mob


def sweep(src, coef, lo, hi, emit):
    chem_lo, mob_lo = chem_mob(src[lo - 2], src[lo - 1], src[lo], coef[lo - 1])
    here, above = src[lo], src[lo + 1]
    chem, mob = chem_mob(src[lo - 1], here, above, coef[lo])
    flux = (mob_lo + mob) * (chem - chem_lo)

    def step(i, state):
        for j in range(2):
            here, above, chem, mob, flux = state
            k = lo + 2 * i + j
            top = src[k + 2]
            chem_up, mob_up = chem_mob(here, above, top, coef[k + 1])
            flux_up = (mob + mob_up) * (chem_up - chem)
            fy = (roll(mob, -1, 0) + mob) * (roll(chem, -1, 0) - chem)
            fx = (roll(mob, -1, 1) + mob) * (roll(chem, -1, 1) - chem)
            total = (flux_up - flux) + (fy - roll(fy, 1, 0)) + (fx - roll(fx, 1, 1))
            emit(k, here, 0.5 * total)
            state = (above, top, chem_up, mob_up, flux_up)
        return state

    lax.fori_loop(0, (hi - lo) // 2, step, (here, above, chem, mob, flux))


def parities(shape):
    rows = lax.broadcasted_iota(jnp.int32, shape, 0)
    cols = lax.broadcasted_iota(jnp.int32, shape, 1)
    return rows % 2 == 0, cols % 2 == 0


def pair(even, a, b, axis):
    kept = jnp.where(even, a, b)
    moved = jnp.where(even, b, a)
    return kept + jnp.where(even, roll(moved, -1, axis), roll(moved, 1, axis))


def pack(src, planes, even_row, even_col):
    sums = [src[2 * q] + src[2 * q + 1] for q in planes]
    upper = pair(even_col, sums[0], sums[1], 1)
    lower = pair(even_col, sums[2], sums[3], 1)
    return 0.125 * pair(even_row, upper, lower, 0)


def unpack(packed, even_row, even_col):
    by_col = (
        jnp.where(even_col, packed, roll(packed, 1, 1)),
        jnp.where(even_col, roll(packed, -1, 1), packed),
    )
    out = []
    for x in by_col:
        out.append(jnp.where(even_row, x, roll(x, 1, 0)))
    for x in by_col:
        out.append(jnp.where(even_row, roll(x, -1, 0), x))
    return out


def coarse_flow(w, coef):
    square = w * w
    around = (roll(w, 2, 0) + roll(w, -2, 0)) + (roll(w, 2, 1) + roll(w, -2, 1))
    chem = w * square - 0.25 * around
    mob = coef * jnp.maximum(1.0 - square, 0.0)
    fy = (roll(mob, -2, 0) + mob) * (roll(chem, -2, 0) - chem)
    fx = (roll(mob, -2, 1) + mob) * (roll(chem, -2, 1) - chem)
    return 0.125 * ((fy - roll(fy, 2, 0)) + (fx - roll(fx, 2, 1)))


def kernel(
    n_tm, n_sp, u_hbm, c_hbm, out, u, c, quad, mid, end, start, node1, node2, mid2, rest,
    forcings, near_send, near_recv, far_send, far_recv, own_sem, tm_send, tm_recv,
):
    planes = u_hbm.shape[0]
    far = HALO - planes
    own = HALO
    t = lax.axis_index("tm")
    s = lax.axis_index("space")
    up, down = lax.rem(s + 1, n_sp), lax.rem(s + n_sp - 1, n_sp)
    up2, down2 = lax.rem(s + 2, n_sp), lax.rem(s + n_sp - 2, n_sp)
    odd = lax.rem(s, 2)
    mate = s + 1 - 2 * odd
    forward = n_sp == 4

    barrier = pltpu.get_barrier_semaphore()
    peers = (up, down) if forward else (up, down, up2, down2)
    for peer in peers:
        pl.semaphore_signal(barrier, inc=1, device_id={"space": peer}, device_id_type=MESH)

    def greet(d, carry):
        pl.semaphore_signal(
            barrier, inc=1, device_id={"tm": lax.rem(t + d, n_tm)}, device_id_type=MESH
        )
        return carry

    lax.fori_loop(1, n_tm, greet, 0)

    local = [
        pltpu.make_async_copy(src, dst.at[pl.ds(own, planes)], own_sem.at[i])
        for i, (src, dst) in enumerate(((u_hbm, u), (c_hbm, c)))
    ]
    for copy in local:
        copy.start()
    pl.semaphore_wait(barrier, len(peers) + n_tm - 1)

    def remote(src, dst, send, recv, peer):
        return pltpu.make_async_remote_copy(
            src_ref=src, dst_ref=dst, send_sem=send, recv_sem=recv,
            device_id={"space": peer}, device_id_type=MESH,
        )

    near = []
    for f, (src, dst) in enumerate(((u_hbm, u), (c_hbm, c))):
        near.append((
            remote(src, dst.at[pl.ds(far, planes)], near_send.at[f, 0], near_recv.at[f, 0], up),
            remote(src, dst.at[pl.ds(own + planes, planes)], near_send.at[f, 1], near_recv.at[f, 1], down),
        ))
        for copy in near[f]:
            copy.start()
    far_copies = []
    if forward:
        cross = odd
        base = far + odd * (own + planes - far)
        for f, dst in enumerate((u, c)):
            remote(
                dst.at[pl.ds(far, planes)], dst.at[pl.ds(far, planes)],
                near_send.at[f, 0], near_recv.at[f, cross], mate,
            ).wait_recv()
            lows = dst.at[pl.ds(base + planes - far, far)]
            highs = dst.at[pl.ds(base, far)]
            for side, (src, at) in enumerate(((lows, 0), (highs, own + 2 * planes))):
                copy = remote(src, dst.at[pl.ds(at, far)], far_send.at[f, side], far_recv.at[f, side], mate)
                copy.start()
                far_copies.append(copy)
        for f, dst in enumerate((u, c)):
            remote(
                dst.at[pl.ds(far, planes)], dst.at[pl.ds(far, planes)],
                near_send.at[f, 0], near_recv.at[f, 1 - cross], mate,
            ).wait_recv()
    else:
        for f, (src, dst) in enumerate(((u_hbm, u), (c_hbm, c))):
            lows = src.at[pl.ds(planes - far, far)]
            highs = src.at[pl.ds(0, far)]
            far_copies.append(remote(lows, dst.at[pl.ds(0, far)], far_send.at[f, 0], far_recv.at[f, 0], up2))
            far_copies.append(remote(highs, dst.at[pl.ds(own + 2 * planes, far)], far_send.at[f, 1], far_recv.at[f, 1], down2))
        for copy in far_copies:
            copy.start()
        for f in range(2):
            for copy in near[f]:
                copy.wait_recv()
    for copy in far_copies:
        copy.wait()
    for f in range(2):
        for copy in near[f]:
            copy.wait_send()
    for copy in local:
        copy.wait()

    total = planes + 2 * HALO
    even_row, even_col = parities(u.shape[1:])

    def emit_mid(k, v, force):
        quad[k] = force
        mid[k] = v + (0.5 * DT) * force

    sweep(u, c, 2, total - 2, emit_mid)

    def emit_end(k, v, force):
        quad[k] = quad[k] + 4.0 * force
        end[k] = v + (0.5 * DT) * force

    sweep(mid, c, 4, total - 4, emit_end)

    def emit_quad(k, v, force):
        quad[k] = quad[k] + force

    sweep(end, c, 6, total - 6, emit_quad)

    mine = list(range(own // 2, (own + planes) // 2))
    others = [q for q in range(3, (total - 6) // 2) if q not in mine]
    groups = []
    for part in (mine, others):
        for i in range(0, len(part), 4):
            group = part[i : i + 4]
            groups.append((group + group + group + group)[:4])
    own_groups = -(-len(mine) // 4)

    coefs = [pack(c, g, even_row, even_col) for g in groups]
    v0 = [pack(u, g, even_row, even_col) for g in groups]
    v1 = [pack(end, g, even_row, even_col) for g in groups]
    force0 = [
        (DT / 6.0) * pack(quad, g, even_row, even_col) - DT * coarse_flow(v, m)
        for g, v, m in zip(groups, v0, coefs)
    ]

    def advance(p, state):
        return tuple(
            w + DT * coarse_flow(w, m) + f for w, m, f in zip(state, coefs, force0)
        )

    w0 = lax.fori_loop(0, t, advance, tuple(v0))
    w1 = advance(0, w0)
    first = t == 0
    for i, g in enumerate(groups):
        by_start = unpack(w0[i] - v1[i], even_row, even_col)
        by_mid = unpack(0.5 * ((w0[i] - v0[i]) + (w1[i] - v1[i])), even_row, even_col)
        by_end = unpack(w1[i] - v1[i], even_row, even_col)
        for j, q in enumerate(g):
            if q in g[:j]:
                continue
            for k in (2 * q, 2 * q + 1):
                start[k] = jnp.where(first, u[k], end[k] + by_start[j])
                node1[k] = mid[k] + by_mid[j]
                node2[k] = end[k] + by_end[j]

    def emit_f0(k, v, force):
        quad[k] = force
        mid2[k] = v + (DT * 5.0 / 24.0) * force
        rest[k] = (-DT / 24.0) * force

    sweep(start, c, 8, total - 8, emit_f0)

    def emit_f1(k, v, force):
        mid2[k] = mid2[k] + (DT / 3.0) * force
        rest[k] = rest[k] - (DT / 6.0) * force

    sweep(node1, c, 8, total - 8, emit_f1)

    def emit_f2(k, v, force):
        mid2[k] = mid2[k] - (DT / 24.0) * force
        rest[k] = rest[k] + (DT * 5.0 / 24.0) * force

    sweep(node2, c, 8, total - 8, emit_f2)

    def emit_end2(k, v, force):
        quad[k] = quad[k] + 4.0 * force
        end[k] = v + (0.5 * DT) * force + rest[k]

    sweep(mid2, c, 10, total - 10, emit_end2)
    sweep(end, c, 12, total - 12, emit_quad)

    for i in range(own_groups):
        g = groups[i]
        before = pack(start, g, even_row, even_col)
        forcings[t, i] = (DT / 6.0) * pack(quad, g, even_row, even_col) - DT * coarse_flow(before, coefs[i])

    def to_slice(d):
        return pltpu.make_async_remote_copy(
            src_ref=forcings.at[t], dst_ref=forcings.at[t],
            send_sem=tm_send.at[d], recv_sem=tm_recv.at[t],
            device_id={"tm": lax.rem(t + d, n_tm)}, device_id_type=MESH,
        )

    def send(i, carry):
        d = n_tm - 1 - i

        @pl.when(t + d < n_tm)
        def _():
            to_slice(d).start()

        return carry

    lax.fori_loop(0, n_tm - 1, send, 0)

    last = [pack(end, g, even_row, even_col) for g in groups[:own_groups]]

    def follow(p, state):
        pltpu.make_async_remote_copy(
            src_ref=forcings.at[p], dst_ref=forcings.at[p],
            send_sem=tm_send.at[0], recv_sem=tm_recv.at[p],
            device_id={"tm": lax.rem(t + 1, n_tm)}, device_id_type=MESH,
        ).wait_recv()
        return tuple(
            w + DT * coarse_flow(w, coefs[i]) + forcings[p, i] for i, w in enumerate(state)
        )

    state = lax.fori_loop(0, t, follow, tuple(v0[:own_groups]))
    for i in range(own_groups):
        w = state[i] + DT * coarse_flow(state[i], coefs[i]) + forcings[t, i]
        fixes = unpack(w - last[i], even_row, even_col)
        for j, q in enumerate(groups[i]):
            for k in (2 * q, 2 * q + 1):
                out[k - own] = end[k] + fixes[j]

    def sent(d, carry):
        @pl.when(t + d < n_tm)
        def _():
            to_slice(d).wait_send()

        return carry

    lax.fori_loop(1, n_tm, sent, 0)


def solution(mesh):
    n_tm, n_sp = mesh.shape["tm"], mesh.shape["space"]

    def on_device(initial_field, mobility):
        planes, rows, cols = initial_field.shape
        wide = pltpu.VMEM((planes + 2 * HALO, rows, cols), jnp.float32)
        out = pl.pallas_call(
            functools.partial(kernel, n_tm, n_sp),
            out_shape=jax.ShapeDtypeStruct(initial_field.shape, jnp.float32),
            in_specs=[pl.BlockSpec(memory_space=pl.ANY)] * 2,
            out_specs=pl.BlockSpec(memory_space=pltpu.VMEM),
            scratch_shapes=[wide] * 10
            + [
                pltpu.VMEM((n_tm, -(-planes // 8), rows, cols), jnp.float32),
                pltpu.SemaphoreType.DMA((2, 2)),
                pltpu.SemaphoreType.DMA((2, 2)),
                pltpu.SemaphoreType.DMA((2, 2)),
                pltpu.SemaphoreType.DMA((2, 2)),
                pltpu.SemaphoreType.DMA((2,)),
                pltpu.SemaphoreType.DMA((n_tm,)),
                pltpu.SemaphoreType.DMA((n_tm,)),
            ],
            compiler_params=pltpu.CompilerParams(
                collective_id=0, has_side_effects=True, vmem_limit_bytes=32 * 2**20
            ),
        )(initial_field, mobility)
        return out[None]

    specs = (P("space", None, None), P("space", None, None))
    return jax.shard_map(
        on_device, mesh=mesh, in_specs=specs, out_specs=P("tm", "space", None, None), check_vma=False
    )
```

```python
import functools

import jax
import jax.numpy as jnp
from jax import lax
from jax.experimental import pallas as pl
from jax.experimental.pallas import tpu as pltpu
from jax.sharding import PartitionSpec as P


DT = 0.016
HALO = 12
MESH = pl.DeviceIdType.MESH


def roll(x, shift, axis):
    return pltpu.roll(x, shift % x.shape[axis], axis)


class Mirrored:
    def __init__(self, ref, origin, sign):
        self.ref, self.origin, self.sign = ref, origin, sign

    def __getitem__(self, k):
        return self.ref[self.origin + self.sign * k]


def chem_mob(below, here, above, coef):
    square = here * here
    around = (
        (below + above)
        + (roll(here, 1, 0) + roll(here, -1, 0))
        + (roll(here, 1, 1) + roll(here, -1, 1))
    )
    chem = here * (square + 5.0) - around
    mob = coef * jnp.maximum(1.0 - square, 0.0)
    return chem, mob


def sweep(src, coef, lo, hi, emit):
    chem_lo, mob_lo = chem_mob(src[lo - 2], src[lo - 1], src[lo], coef[lo - 1])
    here, above = src[lo], src[lo + 1]
    chem, mob = chem_mob(src[lo - 1], here, above, coef[lo])
    flux = (mob_lo + mob) * (chem - chem_lo)

    def step(i, state):
        for j in range(4):
            here, above, chem, mob, flux = state
            k = lo + 4 * i + j
            top = src[k + 2]
            chem_up, mob_up = chem_mob(here, above, top, coef[k + 1])
            flux_up = (mob + mob_up) * (chem_up - chem)
            fy = (roll(mob, -1, 0) + mob) * (roll(chem, -1, 0) - chem)
            fx = (roll(mob, -1, 1) + mob) * (roll(chem, -1, 1) - chem)
            total = (flux_up - flux) + (fy - roll(fy, 1, 0)) + (fx - roll(fx, 1, 1))
            emit(k, here, 0.5 * total)
            state = (above, top, chem_up, mob_up, flux_up)
        return state

    lax.fori_loop(0, (hi - lo) // 4, step, (here, above, chem, mob, flux))


def parities(shape):
    rows = lax.broadcasted_iota(jnp.int32, shape, 0)
    cols = lax.broadcasted_iota(jnp.int32, shape, 1)
    return rows % 2 == 0, cols % 2 == 0


def pair(even, a, b, axis):
    kept = jnp.where(even, a, b)
    moved = jnp.where(even, b, a)
    return kept + jnp.where(even, roll(moved, -1, axis), roll(moved, 1, axis))


def pack(src, planes, even_row, even_col):
    sums = [src[2 * q] + src[2 * q + 1] for q in planes]
    upper = pair(even_col, sums[0], sums[1], 1)
    lower = pair(even_col, sums[2], sums[3], 1)
    return 0.125 * pair(even_row, upper, lower, 0)


def unpack(packed, even_row, even_col):
    by_col = (
        jnp.where(even_col, packed, roll(packed, 1, 1)),
        jnp.where(even_col, roll(packed, -1, 1), packed),
    )
    out = []
    for x in by_col:
        out.append(jnp.where(even_row, x, roll(x, 1, 0)))
    for x in by_col:
        out.append(jnp.where(even_row, roll(x, -1, 0), x))
    return out


def coarse_flow(w, coef):
    square = w * w
    around = (roll(w, 2, 0) + roll(w, -2, 0)) + (roll(w, 2, 1) + roll(w, -2, 1))
    chem = w * square - 0.25 * around
    mob = coef * jnp.maximum(1.0 - square, 0.0)
    fy = (roll(mob, -2, 0) + mob) * (roll(chem, -2, 0) - chem)
    fx = (roll(mob, -2, 1) + mob) * (roll(chem, -2, 1) - chem)
    return 0.125 * ((fy - roll(fy, 2, 0)) + (fx - roll(fx, 2, 1)))


def kernel(
    n_tm, n_sp, u_hbm, c_hbm, out, u, c, quad, mid, end, start, node1, node2, mid2, rest,
    forcings, sp_send, sp_recv, own_sem, tm_send, tm_recv,
):
    planes = u_hbm.shape[0]
    far = HALO - planes
    own = HALO
    t = lax.axis_index("tm")
    s = lax.axis_index("space")
    up, down = lax.rem(s + 1, n_sp), lax.rem(s + n_sp - 1, n_sp)
    up2, down2 = lax.rem(s + 2, n_sp), lax.rem(s + n_sp - 2, n_sp)
    odd = lax.rem(s, 2)
    mate = s + 1 - 2 * odd
    forward = n_sp == 4

    barrier = pltpu.get_barrier_semaphore()
    peers = (up, down) if forward else (up, down, up2, down2)
    for peer in peers:
        pl.semaphore_signal(barrier, inc=1, device_id={"space": peer}, device_id_type=MESH)

    def greet(d, carry):
        pl.semaphore_signal(
            barrier, inc=1, device_id={"tm": lax.rem(t + d, n_tm)}, device_id_type=MESH
        )
        return carry

    lax.fori_loop(1, n_tm, greet, 0)

    local = [
        pltpu.make_async_copy(src, dst.at[pl.ds(own, planes)], own_sem.at[i])
        for i, (src, dst) in enumerate(((u_hbm, u), (c_hbm, c)))
    ]
    for copy in local:
        copy.start()
    pl.semaphore_wait(barrier, len(peers) + n_tm - 1)

    def remote(f, kind, src, src_at, dst_at, rows, peer):
        return pltpu.make_async_remote_copy(
            src_ref=src.at[pl.ds(src_at, rows)], dst_ref=(u, c)[f].at[pl.ds(dst_at, rows)],
            send_sem=sp_send.at[f, kind], recv_sem=sp_recv.at[f, kind],
            device_id={"space": peer}, device_id_type=MESH,
        )

    def pick(even, other):
        return even + odd * (other - even)

    half = planes // 2
    lower, upper = own - planes, own + planes
    inputs = (u_hbm, c_hbm)
    cross = pick(down, up)
    mates, nears, fars, mate_nears, mate_fars = [], [], [], [], []
    for f in range(2):
        nears.append(remote(f, 1, inputs[f], pick(0, half), pick(upper, own - half), half, cross))
    for f in range(2):
        mates.append(remote(f, 0, inputs[f], 0, pick(lower, upper), planes, mate))
    for f in range(2):
        fars.append(remote(f, 2, inputs[f], pick(half, 0), pick(upper + half, lower), half, cross))
    for f in range(2):
        if forward:
            mate_nears.append(remote(f, 3, (u, c)[f], pick(own - half, upper), pick(0, upper + planes), far, mate))
            mate_fars.append(remote(f, 4, (u, c)[f], pick(lower, upper + half), pick(upper + planes, 0), far, mate))
        else:
            mate_nears.append(remote(f, 3, inputs[f], pick(0, planes - far), pick(upper + planes, 0), far, pick(down2, up2)))
            mate_fars.append(remote(f, 4, inputs[f], pick(planes - far, 0), pick(0, upper + planes), far, pick(up2, down2)))
    for copy in nears + mates + fars:
        copy.start()
    if not forward:
        for copy in mate_nears + mate_fars:
            copy.start()

    total = planes + 2 * HALO
    even_row, even_col = parities(u.shape[1:])
    origin, sign = odd * (total - 1), 1 - 2 * odd
    ui, ci = Mirrored(u, origin, sign), Mirrored(c, origin, sign)

    def emit_mid(k, v, force):
        quad[k] = force
        mid[k] = v + (0.5 * DT) * force

    def emit_end(k, v, force):
        quad[k] = quad[k] + 4.0 * force
        end[k] = v + (0.5 * DT) * force

    def emit_quad(k, v, force):
        quad[k] = quad[k] + force

    for copy in local:
        copy.wait()
    for copy in mates:
        copy.wait_recv()
    top = own + 2 * planes
    sweep(ui, ci, own + 2, top - 2, emit_mid)
    sweep(mid, ci, own + 4, top - 4, emit_end)
    sweep(end, ci, own + 6, top - 6, emit_quad)

    for arrived, passed in ((nears, mate_nears), (fars, mate_fars)):
        for i in range(2):
            arrived[i].wait_recv()
            if forward:
                passed[i].start()
        for copy in passed:
            copy.wait_recv()
        if arrived is nears:
            low = own - half
            sweep(ui, ci, low + 2, own + 2, emit_mid)
            sweep(ui, ci, top - 2, top + 2, emit_mid)
            sweep(mid, ci, low + 4, own + 4, emit_end)
            sweep(mid, ci, top - 4, top, emit_end)
            sweep(end, ci, low + 6, own + 6, emit_quad)
            sweep(end, ci, top - 6, top - 2, emit_quad)
        else:
            sweep(ui, ci, 2, low + 2, emit_mid)
            sweep(mid, ci, 4, low + 4, emit_end)
            sweep(end, ci, 6, low + 6, emit_quad)

    mine = list(range(own // 2, (own + planes) // 2))
    others = [q for q in range(3, (total - 6) // 2) if q not in mine]
    groups = []
    for part in (mine, others):
        for i in range(0, len(part), 4):
            group = part[i : i + 4]
            groups.append((group + group + group + group)[:4])
    own_groups = -(-len(mine) // 4)

    coefs = [pack(ci, g, even_row, even_col) for g in groups]
    v0 = [pack(ui, g, even_row, even_col) for g in groups]
    v1 = [pack(end, g, even_row, even_col) for g in groups]
    force0 = [
        (DT / 6.0) * pack(quad, g, even_row, even_col) - DT * coarse_flow(v, m)
        for g, v, m in zip(groups, v0, coefs)
    ]

    def advance(p, state):
        return tuple(
            w + DT * coarse_flow(w, m) + f for w, m, f in zip(state, coefs, force0)
        )

    w0 = lax.fori_loop(0, t, advance, tuple(v0))
    w1 = advance(0, w0)
    first = t == 0
    for i, g in enumerate(groups):
        by_start = unpack(w0[i] - v1[i], even_row, even_col)
        by_mid = unpack(0.5 * ((w0[i] - v0[i]) + (w1[i] - v1[i])), even_row, even_col)
        by_end = unpack(w1[i] - v1[i], even_row, even_col)
        for j, q in enumerate(g):
            if q in g[:j]:
                continue
            for k in (2 * q, 2 * q + 1):
                start[k] = jnp.where(first, ui[k], end[k] + by_start[j])
                node1[k] = mid[k] + by_mid[j]
                node2[k] = end[k] + by_end[j]

    def emit_f0(k, v, force):
        quad[k] = force
        mid2[k] = v + (DT * 5.0 / 24.0) * force
        rest[k] = (-DT / 24.0) * force

    sweep(start, ci, 8, total - 8, emit_f0)

    def emit_f1(k, v, force):
        mid2[k] = mid2[k] + (DT / 3.0) * force
        rest[k] = rest[k] - (DT / 6.0) * force

    sweep(node1, ci, 8, total - 8, emit_f1)

    def emit_f2(k, v, force):
        mid2[k] = mid2[k] - (DT / 24.0) * force
        rest[k] = rest[k] + (DT * 5.0 / 24.0) * force

    sweep(node2, ci, 8, total - 8, emit_f2)

    def emit_end2(k, v, force):
        quad[k] = quad[k] + 4.0 * force
        end[k] = v + (0.5 * DT) * force + rest[k]

    sweep(mid2, ci, 10, total - 10, emit_end2)
    sweep(end, ci, 12, total - 12, emit_quad)

    for i in range(own_groups):
        g = groups[i]
        before = pack(start, g, even_row, even_col)
        forcings[t, i] = (DT / 6.0) * pack(quad, g, even_row, even_col) - DT * coarse_flow(before, coefs[i])

    def to_slice(d):
        return pltpu.make_async_remote_copy(
            src_ref=forcings.at[t], dst_ref=forcings.at[t],
            send_sem=tm_send.at[d], recv_sem=tm_recv.at[t],
            device_id={"tm": lax.rem(t + d, n_tm)}, device_id_type=MESH,
        )

    def send(i, carry):
        d = n_tm - 1 - i

        @pl.when(t + d < n_tm)
        def _():
            to_slice(d).start()

        return carry

    lax.fori_loop(0, n_tm - 1, send, 0)

    last = [pack(end, g, even_row, even_col) for g in groups[:own_groups]]

    def follow(p, state):
        pltpu.make_async_remote_copy(
            src_ref=forcings.at[p], dst_ref=forcings.at[p],
            send_sem=tm_send.at[0], recv_sem=tm_recv.at[p],
            device_id={"tm": lax.rem(t + 1, n_tm)}, device_id_type=MESH,
        ).wait_recv()
        return tuple(
            w + DT * coarse_flow(w, coefs[i]) + forcings[p, i] for i, w in enumerate(state)
        )

    state = lax.fori_loop(0, t, follow, tuple(v0[:own_groups]))
    for i in range(own_groups):
        w = state[i] + DT * coarse_flow(state[i], coefs[i]) + forcings[t, i]
        fixes = unpack(w - last[i], even_row, even_col)
        for j, q in enumerate(groups[i]):
            for k in (2 * q, 2 * q + 1):
                out[origin + sign * k - own] = end[k] + fixes[j]

    def sent(d, carry):
        @pl.when(t + d < n_tm)
        def _():
            to_slice(d).wait_send()

        return carry

    lax.fori_loop(1, n_tm, sent, 0)
    for copy in nears + mates + fars + mate_nears + mate_fars:
        copy.wait_send()


def solution(mesh):
    n_tm, n_sp = mesh.shape["tm"], mesh.shape["space"]

    def on_device(initial_field, mobility):
        planes, rows, cols = initial_field.shape
        wide = pltpu.VMEM((planes + 2 * HALO, rows, cols), jnp.float32)
        out = pl.pallas_call(
            functools.partial(kernel, n_tm, n_sp),
            out_shape=jax.ShapeDtypeStruct(initial_field.shape, jnp.float32),
            in_specs=[pl.BlockSpec(memory_space=pl.ANY)] * 2,
            out_specs=pl.BlockSpec(memory_space=pltpu.VMEM),
            scratch_shapes=[wide] * 10
            + [
                pltpu.VMEM((n_tm, -(-planes // 8), rows, cols), jnp.float32),
                pltpu.SemaphoreType.DMA((2, 5)),
                pltpu.SemaphoreType.DMA((2, 5)),
                pltpu.SemaphoreType.DMA((2,)),
                pltpu.SemaphoreType.DMA((n_tm,)),
                pltpu.SemaphoreType.DMA((n_tm,)),
            ],
            compiler_params=pltpu.CompilerParams(
                collective_id=0, has_side_effects=True, vmem_limit_bytes=32 * 2**20
            ),
        )(initial_field, mobility)
        return out[None]

    specs = (P("space", None, None), P("space", None, None))
    return jax.shard_map(
        on_device, mesh=mesh, in_specs=specs, out_specs=P("tm", "space", None, None), check_vma=False
    )
```

```python
import functools

import jax
import jax.numpy as jnp
from jax import lax
from jax.experimental import pallas as pl
from jax.experimental.pallas import tpu as pltpu
from jax.sharding import PartitionSpec as P


DT = 0.016
HALO = 12
MESH = pl.DeviceIdType.MESH


def roll(x, shift, axis):
    return pltpu.roll(x, shift % x.shape[axis], axis)


class Mirrored:
    def __init__(self, ref, origin, sign):
        self.ref, self.origin, self.sign = ref, origin, sign

    def __getitem__(self, k):
        return self.ref[self.origin + self.sign * k]


def chem_mob(below, here, above, coef):
    square = here * here
    around = (
        (below + above)
        + (roll(here, 1, 0) + roll(here, -1, 0))
        + (roll(here, 1, 1) + roll(here, -1, 1))
    )
    chem = here * (square + 5.0) - around
    mob = coef * jnp.maximum(1.0 - square, 0.0)
    return chem, mob


def sweep(sources, coef, lo, hi, emit, steps=0):
    steps = steps or (8 if (hi - lo) % 8 == 0 else 6 if (hi - lo) % 6 == 0 else 4)
    first = []
    for src in sources:
        chem_lo, mob_lo = chem_mob(src[lo - 2], src[lo - 1], src[lo], coef[lo - 1])
        here, above = src[lo], src[lo + 1]
        chem, mob = chem_mob(src[lo - 1], here, above, coef[lo])
        first.append((here, above, chem, mob, (mob_lo + mob) * (chem - chem_lo)))

    def step(i, states):
        for j in range(steps):
            k = lo + steps * i + j
            coef_up = coef[k + 1]
            after, values, forces = [], [], []
            for src, (here, above, chem, mob, flux) in zip(sources, states):
                top = src[k + 2]
                chem_up, mob_up = chem_mob(here, above, top, coef_up)
                flux_up = (mob + mob_up) * (chem_up - chem)
                fy = (roll(mob, -1, 0) + mob) * (roll(chem, -1, 0) - chem)
                fx = (roll(mob, -1, 1) + mob) * (roll(chem, -1, 1) - chem)
                fx -= (roll(mob, 1, 1) + mob) * (chem - roll(chem, 1, 1))
                total = (flux_up - flux) + (fy - roll(fy, 1, 0)) + fx
                after.append((above, top, chem_up, mob_up, flux_up))
                values.append(here)
                forces.append(0.5 * total)
            emit(k, *values, *forces)
            states = tuple(after)
        return states

    lax.fori_loop(0, (hi - lo) // steps, step, tuple(first))


def parities(shape):
    rows = lax.broadcasted_iota(jnp.int32, shape, 0)
    cols = lax.broadcasted_iota(jnp.int32, shape, 1)
    return rows % 2 == 0, cols % 2 == 0


def pair(even, a, b, axis):
    kept = jnp.where(even, a, b)
    moved = jnp.where(even, b, a)
    return kept + jnp.where(even, roll(moved, -1, axis), roll(moved, 1, axis))


def pack(src, planes, even_row, even_col):
    sums = [src[2 * q] + src[2 * q + 1] for q in planes]
    upper = pair(even_col, sums[0], sums[1], 1)
    lower = pair(even_col, sums[2], sums[3], 1)
    return 0.125 * pair(even_row, upper, lower, 0)


def unpack(packed, even_row, even_col):
    by_col = (
        jnp.where(even_col, packed, roll(packed, 1, 1)),
        jnp.where(even_col, roll(packed, -1, 1), packed),
    )
    out = []
    for x in by_col:
        out.append(jnp.where(even_row, x, roll(x, 1, 0)))
    for x in by_col:
        out.append(jnp.where(even_row, roll(x, -1, 0), x))
    return out


def coarse_sides(coef):
    return coef, roll(coef, 2, 1), roll(coef, -2, 1)


def coarse_chem_mob(left, here, right, coef):
    square = here * here
    around = (left + right) + (roll(here, 2, 0) + roll(here, -2, 0))
    return here * square - 0.25 * around, coef * jnp.maximum(1.0 - square, 0.0)


def coarse_flow(w, coefs):
    left, right = roll(w, 2, 1), roll(w, -2, 1)
    chem, mob = coarse_chem_mob(left, w, right, coefs[0])
    chem_l, mob_l = coarse_chem_mob(roll(w, 4, 1), left, w, coefs[1])
    chem_r, mob_r = coarse_chem_mob(w, right, roll(w, -4, 1), coefs[2])
    fx = (mob_r + mob) * (chem_r - chem) - (mob + mob_l) * (chem - chem_l)
    fy = (roll(mob, -2, 0) + mob) * (roll(chem, -2, 0) - chem)
    return 0.125 * ((fy - roll(fy, 2, 0)) + fx)


def kernel(
    n_tm, n_sp, u_hbm, c_hbm, out, u, c, quad, mid, end, start, node1, node2, mid2, rest,
    forcings, sp_send, sp_recv, own_sem, tm_send, tm_recv,
):
    planes = u_hbm.shape[0]
    far = HALO - planes
    own = HALO
    t = lax.axis_index("tm")
    s = lax.axis_index("space")
    up, down = lax.rem(s + 1, n_sp), lax.rem(s + n_sp - 1, n_sp)
    up2, down2 = lax.rem(s + 2, n_sp), lax.rem(s + n_sp - 2, n_sp)
    odd = lax.rem(s, 2)
    mate = s + 1 - 2 * odd
    forward = n_sp == 4

    barrier = pltpu.get_barrier_semaphore()
    peers = (up, down) if forward else (up, down, up2, down2)
    for peer in peers:
        pl.semaphore_signal(barrier, inc=1, device_id={"space": peer}, device_id_type=MESH)

    def greet(d, carry):
        pl.semaphore_signal(
            barrier, inc=1, device_id={"tm": lax.rem(t + d, n_tm)}, device_id_type=MESH
        )
        return carry

    lax.fori_loop(1, n_tm, greet, 0)

    local = [
        pltpu.make_async_copy(src, dst.at[pl.ds(own, planes)], own_sem.at[i])
        for i, (src, dst) in enumerate(((u_hbm, u), (c_hbm, c)))
    ]
    for copy in local:
        copy.start()
    pl.semaphore_wait(barrier, len(peers) + n_tm - 1)

    def remote(f, kind, src, src_at, dst_at, rows, peer):
        return pltpu.make_async_remote_copy(
            src_ref=src.at[pl.ds(src_at, rows)], dst_ref=(u, c)[f].at[pl.ds(dst_at, rows)],
            send_sem=sp_send.at[f, kind], recv_sem=sp_recv.at[f, kind],
            device_id={"space": peer}, device_id_type=MESH,
        )

    def pick(even, other):
        return even + odd * (other - even)

    half = planes // 2
    lower, upper = own - planes, own + planes
    inputs = (u_hbm, c_hbm)
    cross = pick(down, up)
    mates, nears, fars, mate_nears, mate_fars = [], [], [], [], []
    for f in range(2):
        nears.append(remote(f, 1, inputs[f], pick(0, half), pick(upper, own - half), half, cross))
    for f in range(2):
        mates.append(remote(f, 0, inputs[f], 0, pick(lower, upper), planes, mate))
    for f in range(2):
        fars.append(remote(f, 2, inputs[f], pick(half, 0), pick(upper + half, lower), half, cross))
    for f in range(2):
        if forward:
            mate_nears.append(remote(f, 3, (u, c)[f], pick(own - half, upper), pick(0, upper + planes), far, mate))
            mate_fars.append(remote(f, 4, (u, c)[f], pick(lower, upper + half), pick(upper + planes, 0), far, mate))
        else:
            mate_nears.append(remote(f, 3, inputs[f], pick(0, planes - far), pick(upper + planes, 0), far, pick(down2, up2)))
            mate_fars.append(remote(f, 4, inputs[f], pick(planes - far, 0), pick(0, upper + planes), far, pick(up2, down2)))
    for copy in nears + mates + fars:
        copy.start()
    if not forward:
        for copy in mate_nears + mate_fars:
            copy.start()

    total = planes + 2 * HALO
    even_row, even_col = parities(u.shape[1:])
    origin, sign = odd * (total - 1), 1 - 2 * odd
    ui, ci = Mirrored(u, origin, sign), Mirrored(c, origin, sign)

    def emit_mid(k, v, force):
        quad[k] = force
        mid[k] = v + (0.5 * DT) * force

    def emit_end(k, v, force):
        quad[k] = quad[k] + 4.0 * force
        end[k] = v + (0.5 * DT) * force

    def emit_quad(k, v, force):
        quad[k] = quad[k] + force

    for copy in local:
        copy.wait()
    for copy in mates:
        copy.wait_recv()
    top = own + 2 * planes
    sweep((ui,), ci, own + 2, top - 2, emit_mid)
    sweep((mid,), ci, own + 4, top - 4, emit_end)
    sweep((end,), ci, own + 6, top - 6, emit_quad)

    for arrived, passed in ((nears, mate_nears), (fars, mate_fars)):
        for i in range(2):
            arrived[i].wait_recv()
            if forward:
                passed[i].start()
        for copy in passed:
            copy.wait_recv()
        if arrived is nears:
            low = own - half
            sweep((ui,), ci, low + 2, own + 2, emit_mid)
            sweep((ui,), ci, top - 2, top + 2, emit_mid)
            sweep((mid,), ci, low + 4, own + 4, emit_end)
            sweep((mid,), ci, top - 4, top, emit_end)
            sweep((end,), ci, low + 6, own + 6, emit_quad)
            sweep((end,), ci, top - 6, top - 2, emit_quad)
        else:
            sweep((ui,), ci, 2, low + 2, emit_mid)
            sweep((mid,), ci, 4, low + 4, emit_end)
            sweep((end,), ci, 6, low + 6, emit_quad)

    mine = list(range(own // 2, (own + planes) // 2))
    others = [q for q in range(3, (total - 6) // 2) if q not in mine]
    groups = []
    for part in (mine, others):
        for i in range(0, len(part), 4):
            group = part[i : i + 4]
            groups.append((group + group + group + group)[:4])
    own_groups = -(-len(mine) // 4)

    coefs = [coarse_sides(pack(ci, g, even_row, even_col)) for g in groups]
    v0 = [pack(ui, g, even_row, even_col) for g in groups]
    v1 = [pack(end, g, even_row, even_col) for g in groups]
    force0 = [
        (DT / 6.0) * pack(quad, g, even_row, even_col) - DT * coarse_flow(v, m)
        for g, v, m in zip(groups, v0, coefs)
    ]

    def advance(p, state):
        return tuple(
            w + DT * coarse_flow(w, m) + f for w, m, f in zip(state, coefs, force0)
        )

    w0 = lax.fori_loop(0, t, advance, tuple(v0))
    w1 = advance(0, w0)
    first = t == 0
    for i, g in enumerate(groups):
        by_start = unpack(w0[i] - v1[i], even_row, even_col)
        by_mid = unpack(0.5 * ((w0[i] - v0[i]) + (w1[i] - v1[i])), even_row, even_col)
        by_end = unpack(w1[i] - v1[i], even_row, even_col)
        for j, q in enumerate(g):
            if q in g[:j]:
                continue
            for k in (2 * q, 2 * q + 1):
                start[k] = jnp.where(first, ui[k], end[k] + by_start[j])
                node1[k] = mid[k] + by_mid[j]
                node2[k] = end[k] + by_end[j]

    def emit_mid2(k, v, _, __, f0, f1, f2):
        quad[k] = f0
        mid2[k] = v + ((DT * 5.0 / 24.0) * f0 + (DT / 3.0) * f1 - (DT / 24.0) * f2)
        rest[k] = (DT * 5.0 / 24.0) * f2 - (DT / 24.0) * f0 - (DT / 6.0) * f1

    sweep((start, node1, node2), ci, 8, total - 8, emit_mid2, 2)

    def emit_end2(k, v, force):
        quad[k] = quad[k] + 4.0 * force
        end[k] = v + (0.5 * DT) * force + rest[k]

    sweep((mid2,), ci, 10, total - 10, emit_end2)
    sweep((end,), ci, 12, total - 12, emit_quad)

    for i in range(own_groups):
        g = groups[i]
        before = pack(start, g, even_row, even_col)
        forcings[t, i] = (DT / 6.0) * pack(quad, g, even_row, even_col) - DT * coarse_flow(before, coefs[i])

    def to_slice(d):
        return pltpu.make_async_remote_copy(
            src_ref=forcings.at[t], dst_ref=forcings.at[t],
            send_sem=tm_send.at[d], recv_sem=tm_recv.at[t],
            device_id={"tm": lax.rem(t + d, n_tm)}, device_id_type=MESH,
        )

    def send(i, carry):
        d = n_tm - 1 - i

        @pl.when(t + d < n_tm)
        def _():
            to_slice(d).start()

        return carry

    lax.fori_loop(0, n_tm - 1, send, 0)

    last = [pack(end, g, even_row, even_col) for g in groups[:own_groups]]

    def follow(p, state):
        pltpu.make_async_remote_copy(
            src_ref=forcings.at[p], dst_ref=forcings.at[p],
            send_sem=tm_send.at[0], recv_sem=tm_recv.at[p],
            device_id={"tm": lax.rem(t + 1, n_tm)}, device_id_type=MESH,
        ).wait_recv()
        return tuple(
            w + DT * coarse_flow(w, coefs[i]) + forcings[p, i] for i, w in enumerate(state)
        )

    state = lax.fori_loop(0, t, follow, tuple(v0[:own_groups]))
    for i in range(own_groups):
        w = state[i] + DT * coarse_flow(state[i], coefs[i]) + forcings[t, i]
        fixes = unpack(w - last[i], even_row, even_col)
        for j, q in enumerate(groups[i]):
            for k in (2 * q, 2 * q + 1):
                out[origin + sign * k - own] = end[k] + fixes[j]

    def sent(d, carry):
        @pl.when(t + d < n_tm)
        def _():
            to_slice(d).wait_send()

        return carry

    lax.fori_loop(1, n_tm, sent, 0)
    for copy in nears + mates + fars + mate_nears + mate_fars:
        copy.wait_send()


def solution(mesh):
    n_tm, n_sp = mesh.shape["tm"], mesh.shape["space"]

    def on_device(initial_field, mobility):
        planes, rows, cols = initial_field.shape
        wide = pltpu.VMEM((planes + 2 * HALO, rows, cols), jnp.float32)
        out = pl.pallas_call(
            functools.partial(kernel, n_tm, n_sp),
            out_shape=jax.ShapeDtypeStruct(initial_field.shape, jnp.float32),
            in_specs=[pl.BlockSpec(memory_space=pl.ANY)] * 2,
            out_specs=pl.BlockSpec(memory_space=pltpu.VMEM),
            scratch_shapes=[wide] * 10
            + [
                pltpu.VMEM((n_tm, -(-planes // 8), rows, cols), jnp.float32),
                pltpu.SemaphoreType.DMA((2, 5)),
                pltpu.SemaphoreType.DMA((2, 5)),
                pltpu.SemaphoreType.DMA((2,)),
                pltpu.SemaphoreType.DMA((n_tm,)),
                pltpu.SemaphoreType.DMA((n_tm,)),
            ],
            compiler_params=pltpu.CompilerParams(
                collective_id=0, has_side_effects=True, vmem_limit_bytes=32 * 2**20
            ),
        )(initial_field, mobility)
        return out[None]

    specs = (P("space", None, None), P("space", None, None))
    return jax.shard_map(
        on_device, mesh=mesh, in_specs=specs, out_specs=P("tm", "space", None, None), check_vma=False
    )
```

```python
import functools

import jax
import jax.numpy as jnp
from jax import lax
from jax.experimental import pallas as pl
from jax.experimental.pallas import tpu as pltpu
from jax.sharding import PartitionSpec as P


DT = 0.016
HALO = 12
MESH = pl.DeviceIdType.MESH


def roll(x, shift, axis):
    return pltpu.roll(x, shift % x.shape[axis], axis)


class Mirrored:
    def __init__(self, ref, origin, sign):
        self.ref, self.origin, self.sign = ref, origin, sign

    def __getitem__(self, k):
        return self.ref[self.origin + self.sign * k]


def chem_mob(below, here, above, coef):
    square = here * here
    around = (
        (below + above)
        + (roll(here, 1, 0) + roll(here, -1, 0))
        + (roll(here, 1, 1) + roll(here, -1, 1))
    )
    chem = here * (square + 5.0) - around
    mob = coef * jnp.maximum(1.0 - square, 0.0)
    return chem, mob


def sweep(sources, coef, lo, hi, emit, steps=0):
    steps = steps or (8 if (hi - lo) % 8 == 0 else 6 if (hi - lo) % 6 == 0 else 4)
    first = []
    for src in sources:
        chem_lo, mob_lo = chem_mob(src[lo - 2], src[lo - 1], src[lo], coef[lo - 1])
        here, above = src[lo], src[lo + 1]
        chem, mob = chem_mob(src[lo - 1], here, above, coef[lo])
        first.append((here, above, chem, mob, (mob_lo + mob) * (chem - chem_lo)))

    def step(i, states):
        for j in range(steps):
            k = lo + steps * i + j
            coef_up = coef[k + 1]
            after, values, forces = [], [], []
            for src, (here, above, chem, mob, flux) in zip(sources, states):
                top = src[k + 2]
                chem_up, mob_up = chem_mob(here, above, top, coef_up)
                flux_up = (mob + mob_up) * (chem_up - chem)
                fy = (roll(mob, -1, 0) + mob) * (roll(chem, -1, 0) - chem)
                fx = (roll(mob, -1, 1) + mob) * (roll(chem, -1, 1) - chem)
                fx -= (roll(mob, 1, 1) + mob) * (chem - roll(chem, 1, 1))
                total = (flux_up - flux) + (fy - roll(fy, 1, 0)) + fx
                after.append((above, top, chem_up, mob_up, flux_up))
                values.append(here)
                forces.append(0.5 * total)
            emit(k, *values, *forces)
            states = tuple(after)
        return states

    lax.fori_loop(0, (hi - lo) // steps, step, tuple(first))


def parities(shape):
    rows = lax.broadcasted_iota(jnp.int32, shape, 0)
    cols = lax.broadcasted_iota(jnp.int32, shape, 1)
    return rows % 2 == 0, cols % 2 == 0


def pair(even, a, b, axis):
    kept = jnp.where(even, a, b)
    moved = jnp.where(even, b, a)
    return kept + jnp.where(even, roll(moved, -1, axis), roll(moved, 1, axis))


def pack(src, planes, even_row, even_col):
    sums = [src[2 * q] + src[2 * q + 1] for q in planes]
    upper = pair(even_col, sums[0], sums[1], 1)
    lower = pair(even_col, sums[2], sums[3], 1)
    return 0.125 * pair(even_row, upper, lower, 0)


def unpack(packed, even_row, even_col):
    by_col = (
        jnp.where(even_col, packed, roll(packed, 1, 1)),
        jnp.where(even_col, roll(packed, -1, 1), packed),
    )
    out = []
    for x in by_col:
        out.append(jnp.where(even_row, x, roll(x, 1, 0)))
    for x in by_col:
        out.append(jnp.where(even_row, roll(x, -1, 0), x))
    return out


def coarse_sides(coef):
    return coef, roll(coef, 2, 1), roll(coef, -2, 1)


def coarse_chem_mob(left, here, right, coef):
    square = here * here
    around = (left + right) + (roll(here, 2, 0) + roll(here, -2, 0))
    return here * square - 0.25 * around, coef * jnp.maximum(1.0 - square, 0.0)


def coarse_flow(w, coefs):
    left, right = roll(w, 2, 1), roll(w, -2, 1)
    chem, mob = coarse_chem_mob(left, w, right, coefs[0])
    chem_l, mob_l = coarse_chem_mob(roll(w, 4, 1), left, w, coefs[1])
    chem_r, mob_r = coarse_chem_mob(w, right, roll(w, -4, 1), coefs[2])
    fx = (mob_r + mob) * (chem_r - chem) - (mob + mob_l) * (chem - chem_l)
    fy = (roll(mob, -2, 0) + mob) * (roll(chem, -2, 0) - chem)
    return 0.125 * ((fy - roll(fy, 2, 0)) + fx)


def kernel(
    n_tm, n_sp, u_hbm, c_hbm, out, u, c, quad, mid, end, start, node1, node2, mid2, rest,
    forcings, sp_send, sp_recv, own_sem, round_sem, tm_send, tm_recv,
):
    planes = u_hbm.shape[0]
    far = HALO - planes
    own = HALO
    t = lax.axis_index("tm")
    s = lax.axis_index("space")
    up, down = lax.rem(s + 1, n_sp), lax.rem(s + n_sp - 1, n_sp)
    up2, down2 = lax.rem(s + 2, n_sp), lax.rem(s + n_sp - 2, n_sp)
    odd = lax.rem(s, 2)
    mate = s + 1 - 2 * odd
    forward = n_sp == 4

    barrier = pltpu.get_barrier_semaphore()
    peers = (up, down) if forward else (up, down, up2, down2)
    for peer in peers:
        pl.semaphore_signal(barrier, inc=1, device_id={"space": peer}, device_id_type=MESH)

    def greet(sem, d):
        @pl.when(t >= d)
        def _():
            pl.semaphore_signal(sem, inc=1, device_id={"tm": t - d}, device_id_type=MESH)

        @pl.when(t + d < n_tm)
        def _():
            pl.semaphore_signal(sem, inc=1, device_id={"tm": t + d}, device_id_type=MESH)

    def greeted(d):
        return (t >= d).astype(jnp.int32) + (t + d < n_tm).astype(jnp.int32)

    greet(barrier, 1)

    local = [
        pltpu.make_async_copy(src, dst.at[pl.ds(own, planes)], own_sem.at[i])
        for i, (src, dst) in enumerate(((u_hbm, u), (c_hbm, c)))
    ]
    for copy in local:
        copy.start()
    pl.semaphore_wait(barrier, len(peers) + greeted(1))
    rounds = []
    while 2**len(rounds) < n_tm - 1:
        rounds.append(2**len(rounds))
    greet(round_sem.at[0], 1)

    def next_round(r):
        if r < len(rounds):
            pl.semaphore_wait(round_sem.at[r], greeted(rounds[r]))
            if r + 1 < len(rounds):
                greet(round_sem.at[r + 1], rounds[r + 1])

    def remote(f, kind, src, src_at, dst_at, rows, peer):
        return pltpu.make_async_remote_copy(
            src_ref=src.at[pl.ds(src_at, rows)], dst_ref=(u, c)[f].at[pl.ds(dst_at, rows)],
            send_sem=sp_send.at[f, kind], recv_sem=sp_recv.at[f, kind],
            device_id={"space": peer}, device_id_type=MESH,
        )

    def pick(even, other):
        return even + odd * (other - even)

    half = planes // 2
    lower, upper = own - planes, own + planes
    inputs = (u_hbm, c_hbm)
    cross = pick(down, up)
    mates, nears, fars, mate_nears, mate_fars = [], [], [], [], []
    for f in range(2):
        nears.append(remote(f, 1, inputs[f], pick(0, half), pick(upper, own - half), half, cross))
    for f in range(2):
        mates.append(remote(f, 0, inputs[f], 0, pick(lower, upper), planes, mate))
    for f in range(2):
        fars.append(remote(f, 2, inputs[f], pick(half, 0), pick(upper + half, lower), half, cross))
    for f in range(2):
        if forward:
            mate_nears.append(remote(f, 3, (u, c)[f], pick(own - half, upper), pick(0, upper + planes), far, mate))
            mate_fars.append(remote(f, 4, (u, c)[f], pick(lower, upper + half), pick(upper + planes, 0), far, mate))
        else:
            mate_nears.append(remote(f, 3, inputs[f], pick(0, planes - far), pick(upper + planes, 0), far, pick(down2, up2)))
            mate_fars.append(remote(f, 4, inputs[f], pick(planes - far, 0), pick(0, upper + planes), far, pick(up2, down2)))
    for copy in nears + mates + fars:
        copy.start()
    if not forward:
        for copy in mate_nears + mate_fars:
            copy.start()

    total = planes + 2 * HALO
    even_row, even_col = parities(u.shape[1:])
    origin, sign = odd * (total - 1), 1 - 2 * odd
    ui, ci = Mirrored(u, origin, sign), Mirrored(c, origin, sign)

    def emit_mid(k, v, force):
        quad[k] = force
        mid[k] = v + (0.5 * DT) * force

    def emit_end(k, v, force):
        quad[k] = quad[k] + 4.0 * force
        end[k] = v + (0.5 * DT) * force

    def emit_quad(k, v, force):
        quad[k] = quad[k] + force

    for copy in local:
        copy.wait()
    for copy in mates:
        copy.wait_recv()
    top = own + 2 * planes
    sweep((ui,), ci, own + 2, top - 2, emit_mid)
    sweep((mid,), ci, own + 4, top - 4, emit_end)
    sweep((end,), ci, own + 6, top - 6, emit_quad)
    next_round(0)

    for arrived, passed in ((nears, mate_nears), (fars, mate_fars)):
        for i in range(2):
            arrived[i].wait_recv()
            if forward:
                passed[i].start()
        for copy in passed:
            copy.wait_recv()
        if arrived is nears:
            low = own - half
            sweep((ui,), ci, low + 2, own + 2, emit_mid)
            sweep((ui,), ci, top - 2, top + 2, emit_mid)
            sweep((mid,), ci, low + 4, own + 4, emit_end)
            sweep((mid,), ci, top - 4, top, emit_end)
            sweep((end,), ci, low + 6, own + 6, emit_quad)
            sweep((end,), ci, top - 6, top - 2, emit_quad)
            next_round(1)
        else:
            sweep((ui,), ci, 2, low + 2, emit_mid)
            sweep((mid,), ci, 4, low + 4, emit_end)
            sweep((end,), ci, 6, low + 6, emit_quad)

    mine = list(range(own // 2, (own + planes) // 2))
    others = [q for q in range(3, (total - 6) // 2) if q not in mine]
    groups = []
    for part in (mine, others):
        for i in range(0, len(part), 4):
            group = part[i : i + 4]
            groups.append((group + group + group + group)[:4])
    own_groups = -(-len(mine) // 4)

    coefs = [coarse_sides(pack(ci, g, even_row, even_col)) for g in groups]
    v0 = [pack(ui, g, even_row, even_col) for g in groups]
    v1 = [pack(end, g, even_row, even_col) for g in groups]
    force0 = [
        (DT / 6.0) * pack(quad, g, even_row, even_col) - DT * coarse_flow(v, m)
        for g, v, m in zip(groups, v0, coefs)
    ]

    def advance(p, state):
        return tuple(
            w + DT * coarse_flow(w, m) + f for w, m, f in zip(state, coefs, force0)
        )

    w0 = lax.fori_loop(0, t, advance, tuple(v0))
    w1 = advance(0, w0)
    first = t == 0
    for i, g in enumerate(groups):
        by_start = unpack(w0[i] - v1[i], even_row, even_col)
        by_mid = unpack(0.5 * ((w0[i] - v0[i]) + (w1[i] - v1[i])), even_row, even_col)
        by_end = unpack(w1[i] - v1[i], even_row, even_col)
        for j, q in enumerate(g):
            if q in g[:j]:
                continue
            for k in (2 * q, 2 * q + 1):
                start[k] = jnp.where(first, ui[k], end[k] + by_start[j])
                node1[k] = mid[k] + by_mid[j]
                node2[k] = end[k] + by_end[j]

    def emit_mid2(k, v, _, __, f0, f1, f2):
        quad[k] = f0
        mid2[k] = v + ((DT * 5.0 / 24.0) * f0 + (DT / 3.0) * f1 - (DT / 24.0) * f2)
        rest[k] = (DT * 5.0 / 24.0) * f2 - (DT / 24.0) * f0 - (DT / 6.0) * f1

    sweep((start, node1, node2), ci, 8, total - 8, emit_mid2, 2)

    def emit_end2(k, v, force):
        quad[k] = quad[k] + 4.0 * force
        end[k] = v + (0.5 * DT) * force + rest[k]

    for r in range(2, len(rounds)):
        next_round(r)
    sweep((mid2,), ci, 10, total - 10, emit_end2)
    sweep((end,), ci, 12, total - 12, emit_quad)

    for i in range(own_groups):
        g = groups[i]
        before = pack(start, g, even_row, even_col)
        forcings[t, i] = (DT / 6.0) * pack(quad, g, even_row, even_col) - DT * coarse_flow(before, coefs[i])

    def to_slice(d):
        return pltpu.make_async_remote_copy(
            src_ref=forcings.at[t], dst_ref=forcings.at[t],
            send_sem=tm_send.at[d], recv_sem=tm_recv.at[t],
            device_id={"tm": lax.rem(t + d, n_tm)}, device_id_type=MESH,
        )

    def send(i, carry):
        d = n_tm - 1 - i

        @pl.when(t + d < n_tm)
        def _():
            to_slice(d).start()

        return carry

    lax.fori_loop(0, n_tm - 1, send, 0)

    last = [pack(end, g, even_row, even_col) for g in groups[:own_groups]]

    def follow(p, state):
        pltpu.make_async_remote_copy(
            src_ref=forcings.at[p], dst_ref=forcings.at[p],
            send_sem=tm_send.at[0], recv_sem=tm_recv.at[p],
            device_id={"tm": lax.rem(t + 1, n_tm)}, device_id_type=MESH,
        ).wait_recv()
        return tuple(
            w + DT * coarse_flow(w, coefs[i]) + forcings[p, i] for i, w in enumerate(state)
        )

    state = lax.fori_loop(0, t, follow, tuple(v0[:own_groups]))
    for i in range(own_groups):
        w = state[i] + DT * coarse_flow(state[i], coefs[i]) + forcings[t, i]
        fixes = unpack(w - last[i], even_row, even_col)
        for j, q in enumerate(groups[i]):
            for k in (2 * q, 2 * q + 1):
                out[origin + sign * k - own] = end[k] + fixes[j]

    def sent(d, carry):
        @pl.when(t + d < n_tm)
        def _():
            to_slice(d).wait_send()

        return carry

    lax.fori_loop(1, n_tm, sent, 0)
    for copy in nears + mates + fars + mate_nears + mate_fars:
        copy.wait_send()


def solution(mesh):
    n_tm, n_sp = mesh.shape["tm"], mesh.shape["space"]

    def on_device(initial_field, mobility):
        planes, rows, cols = initial_field.shape
        wide = pltpu.VMEM((planes + 2 * HALO, rows, cols), jnp.float32)
        out = pl.pallas_call(
            functools.partial(kernel, n_tm, n_sp),
            out_shape=jax.ShapeDtypeStruct(initial_field.shape, jnp.float32),
            in_specs=[pl.BlockSpec(memory_space=pl.ANY)] * 2,
            out_specs=pl.BlockSpec(memory_space=pltpu.VMEM),
            scratch_shapes=[wide] * 10
            + [
                pltpu.VMEM((n_tm, -(-planes // 8), rows, cols), jnp.float32),
                pltpu.SemaphoreType.DMA((2, 5)),
                pltpu.SemaphoreType.DMA((2, 5)),
                pltpu.SemaphoreType.DMA((2,)),
                pltpu.SemaphoreType.REGULAR((max(1, (n_tm - 1).bit_length()),)),
                pltpu.SemaphoreType.DMA((n_tm,)),
                pltpu.SemaphoreType.DMA((n_tm,)),
            ],
            compiler_params=pltpu.CompilerParams(
                collective_id=0, has_side_effects=True, vmem_limit_bytes=32 * 2**20
            ),
        )(initial_field, mobility)
        return out[None]

    specs = (P("space", None, None), P("space", None, None))
    return jax.shard_map(
        on_device, mesh=mesh, in_specs=specs, out_specs=P("tm", "space", None, None), check_vma=False
    )
```
